32 devices in a mesh: inline: 8 (over z, core), xline: 4 (over y, x).
Axes of the slice: x: 2, y: 2, z: 4, core: 2. Of those that a mesh axis runs over, the one named last changes fastest.
Arguments:
- probes: float32 [2, 128, 128, 128], P(None, 'inline', 'xline'), may hold values from -6 to 6
- diffusion: bfloat16 [3, 128, 128, 128], P(None, 'inline', 'xline'), may hold values from -1 to 1, as said below
- wavelet: float32 [41], replicated, may hold values from -1 to 1
Outputs:
- iterate: float32 [2, 128, 128, 128], P(None, 'inline', 'xline')
The draws below stay inside these ranges and needn't reach their ends.
Inputs may be any that keep to these rules, and one draw needn't show every extreme that they name: `diffusion`: components 0 and 2 are positive; component 1 lies within nine tenths of the root of their product in magnitude.
All inputs are finite; a program needn't handle non-finite values.
Results may differ from the reference program's by a relative error of at most 0.0003.
Values may be sent and summed in bfloat16 or wider, within the bound.
A program may use at most 64 MiB of HBM per device.

```python
import jax
import jax.numpy as jnp
from jax import lax

NT = 128
HALF = 20
TAPS = 41
PAIRS = 3
NV = 2
NI = 128
NX = 128


def draw_diffusion(key, part):
    first_key, second_key, third_key = jax.random.split(jax.random.fold_in(key, 17), 3)
    shape = (NI, NX, NT)
    lower, upper = (0.05, 0.5)
    span_low = jnp.log(jnp.float32(lower))
    span_high = jnp.log(jnp.float32(upper))
    coef_in = jnp.exp(jax.random.uniform(first_key, shape, jnp.float32, span_low, span_high))
    coef_x = jnp.exp(jax.random.uniform(second_key, shape, jnp.float32, span_low, span_high))
    shear = jax.random.uniform(third_key, shape, jnp.float32, -0.9, 0.9)
    coef_mix = shear * jnp.sqrt(coef_in * coef_x)
    return jnp.stack([coef_in, coef_mix, coef_x]).astype(jnp.bfloat16)


def level_of(stream_key, dims, shards, smallest, largest):
    level = 1.0
    for dim, parts in shards:
        steps = jax.random.uniform(jax.random.fold_in(jax.random.fold_in(stream_key, 6), dim), (parts,), jnp.float32, smallest / len(shards), largest / len(shards))
        level = level * jnp.repeat(jnp.exp(steps), dims[dim] // parts).reshape((-1,) + (1,) * (len(dims) - 1 - dim))
    return level


def noise(key, shape, scale, limit, cuts=(), dtype=jnp.bfloat16):
    result = jax.random.normal(key, shape, jnp.float32) * scale
    if len(cuts) > 0:
        result = level_of(key, shape, cuts, -0.22, 0.18) * result
    return jnp.clip(result, min=-limit, max=limit).astype(dtype)


def setup_inputs(seed: int = 0) -> dict:
    seeds = jax.random.split(jax.random.key(seed), 4)
    return {
        "probes": noise(seeds[0], (NV, NI, NX, NT), 1.0, 6.0, ((1, 8), (2, 4)), jnp.float32),
        "diffusion": draw_diffusion(jax.random.fold_in(seeds[3], 71), 0),
        "wavelet": noise(seeds[2], (TAPS,), TAPS ** -0.5, 1.0, (), jnp.float32),
    }


def wavelet_matrix(wavelet):
    offset = jnp.arange(NT)[None, :] - jnp.arange(NT)[:, None] + HALF
    onehot = (offset[:, :, None] == jnp.arange(2 * HALF + 1)[None, None, :]).astype(jnp.float32)
    return jnp.einsum("stk,k->st", onehot, wavelet.astype(jnp.float32), precision=lax.Precision.HIGHEST)


def data_term(volume, matrix):
    shape = volume.shape
    trace_rows = volume.reshape(-1, shape[-1])
    convolved = jnp.dot(trace_rows, matrix, precision=lax.Precision.HIGHEST)
    return jnp.dot(convolved, matrix.T, precision=lax.Precision.HIGHEST).reshape(shape)


def regularize(volume, tensor):
    padded = jnp.pad(volume, ((0, 1), (0, 1), (0, 0)))
    step_in = padded[1:, :-1] - volume
    step_x = padded[:-1, 1:] - volume
    flux_in = tensor[0] * step_in + tensor[1] * step_x
    flux_x = tensor[1] * step_in + tensor[2] * step_x
    lower_in = jnp.pad(flux_in, ((1, 0), (0, 0), (0, 0)))[:-1]
    lower_x = jnp.pad(flux_x, ((0, 0), (1, 0), (0, 0)))[:, :-1]
    return (lower_in - flux_in) + (lower_x - flux_x)


def reference(probes, diffusion, wavelet):
    matrix = wavelet_matrix(wavelet)
    tensor = diffusion.astype(jnp.float32)

    def damped(volume):
        return volume - 0.25 * (data_term(volume, matrix) + regularize(volume, tensor))

    def repeated(volume):
        for turn in range(2 * PAIRS):
            volume = damped(volume)
        return volume

    return lax.map(repeated, probes)
```

```python
import functools

import jax
import jax.numpy as jnp
from jax import lax
from jax.experimental import pallas as pl
from jax.experimental.pallas import tpu as pltpu
from jax.sharding import PartitionSpec as P

STEPS = 6
WIDTH = 2
ROUNDS = STEPS // WIDTH
DAMPING = 0.25
VECTORS = 2
PLANES = VECTORS + 3
LANES = 128
SUB = 8
WAYS = ((-1, 0), (1, 0), (0, -1), (0, 1), (-1, -1), (-1, 1), (1, -1), (1, 1))


def kernel(probes, diffusion, wavelet, out, *scratch):
    H = WIDTH
    nv, I, J, S = probes.shape
    C = J + SUB
    R = I + 2 * H
    at = 0

    def take(count):
        nonlocal at
        at += count
        return scratch[at - count:at]

    xs = take(ROUNDS)
    ys = take(ROUNDS * (H - 1))
    east_out = take(ROUNDS)
    west_out = take(ROUNDS)
    east_in = take(ROUNDS)
    west_in = take(ROUNDS)
    raw, smooth, mat, load_sem, send_sem, recv_sem = take(6)

    me_in = lax.axis_index("inline")
    me_x = lax.axis_index("xline")
    n_in = lax.axis_size("inline")
    n_x = lax.axis_size("xline")
    has = {
        (-1, 0): me_in > 0,
        (1, 0): me_in < n_in - 1,
        (0, -1): me_x > 0,
        (0, 1): me_x < n_x - 1,
    }
    for di, dx in WAYS[4:]:
        has[(di, dx)] = jnp.logical_and(has[(di, 0)], has[(0, dx)])

    def device(way):
        return {"inline": me_in + way[0], "xline": me_x + way[1]}

    loads = [
        pltpu.make_async_copy(diffusion, raw, load_sem.at[0]),
        pltpu.make_async_copy(probes.at[0], xs[0].at[1, H:H + I, 0:J], load_sem.at[1]),
        pltpu.make_async_copy(probes.at[1], xs[0].at[0, H:H + I, 0:J], load_sem.at[2]),
    ]
    for load in loads:
        load.start()

    barrier = pltpu.get_barrier_semaphore()
    for way in WAYS:
        @pl.when(has[way])
        def _(way=way):
            pl.semaphore_signal(
                barrier, inc=1, device_id=device(way), device_id_type=pl.DeviceIdType.MESH
            )

    for r in range(ROUNDS):
        for side, rows in (((-1, 0), slice(0, H)), ((1, 0), slice(H + I, R))):
            @pl.when(jnp.logical_not(has[side]))
            def _(r=r, rows=rows):
                planes = xs[r].shape[0]
                xs[r][:, rows, 0:J] = jnp.zeros((planes, H, J, S), jnp.float32)
                east_in[r][:, rows] = jnp.zeros((planes, H, H, S), jnp.float32)
                west_in[r][:, rows] = jnp.zeros((planes, H, H, S), jnp.float32)
        for side, buffer in (((0, 1), east_in[r]), ((0, -1), west_in[r])):
            @pl.when(jnp.logical_not(has[side]))
            def _(buffer=buffer):
                buffer[...] = jnp.zeros(buffer.shape, jnp.float32)

    neighbours = (
        (1 + has[(-1, 0)].astype(jnp.int32) + has[(1, 0)].astype(jnp.int32))
        * (1 + has[(0, -1)].astype(jnp.int32) + has[(0, 1)].astype(jnp.int32))
        - 1
    )

    def copies(r, group, planes):
        x = xs[r]
        p = slice(*planes)
        low, high = slice(0, H), slice(H + I, R)
        middle = slice(H, H + I)
        ends = {
            (-1, 0): (x.at[p, H:2 * H, 0:J], x.at[p, high, 0:J]),
            (1, 0): (x.at[p, I:I + H, 0:J], x.at[p, low, 0:J]),
            (0, -1): (west_out[r].at[p], east_in[r].at[p, middle]),
            (0, 1): (east_out[r].at[p], west_in[r].at[p, middle]),
            (-1, -1): (west_out[r].at[p, 0:H], east_in[r].at[p, high]),
            (-1, 1): (east_out[r].at[p, 0:H], west_in[r].at[p, high]),
            (1, -1): (west_out[r].at[p, I - H:I], east_in[r].at[p, low]),
            (1, 1): (east_out[r].at[p, I - H:I], west_in[r].at[p, low]),
        }
        return {
            way: pltpu.make_async_remote_copy(
                src_ref=ends[way][0],
                dst_ref=ends[way][1],
                send_sem=send_sem.at[r, group, k],
                recv_sem=recv_sem.at[r, group, k],
                device_id=device(way),
                device_id_type=pl.DeviceIdType.MESH,
            )
            for k, way in enumerate(WAYS)
        }

    def planes_of(r, group):
        if group == 1:
            return (0, 1)
        return (1, PLANES) if r == 0 else (1, 2)

    def pack(r, planes):
        for p in range(*planes):
            def body(i, carry, p=p):
                west_out[r][p, i] = xs[r][p, H + i, 0:H]
                east_out[r][p, i] = xs[r][p, H + i, J - H:J]
                return carry
            lax.fori_loop(0, I, body, 0)

    def send(r, group):
        made = copies(r, group, planes_of(r, group))
        for way in WAYS:
            @pl.when(has[way])
            def _(way=way):
                made[way].start()

    def receive(r, group):
        planes = planes_of(r, group)
        made = copies(r, group, planes)
        for way in WAYS:
            @pl.when(has[(-way[0], -way[1])])
            def _(way=way):
                made[way].wait_recv()
        for p in range(*planes):
            def body(i, carry, p=p):
                xs[r][p, i, J:J + H] = east_in[r][p, i]
                xs[r][p, i, C - H:C] = west_in[r][p, i]
                return carry
            lax.fori_loop(0, R, body, 0)

    def step(src, dst, plane, low, high, store):
        rows = (high - low) * C
        block = src[plane, low:high].reshape(rows, S)
        top = block.astype(jnp.bfloat16)
        rest = (block - top.astype(jnp.float32)).astype(jnp.bfloat16)
        both = jnp.dot(
            jnp.concatenate([top, rest], axis=1), mat[...], preferred_element_type=jnp.float32
        )
        smooth[low:high] = (both[:, :S] + both[:, S:]).reshape(high - low, C, S)
        tensor = xs[0]

        def flux(i, here):
            below = src[plane, i + 1]
            a, b, c = tensor[VECTORS, i], tensor[VECTORS + 1, i], tensor[VECTORS + 2, i]
            step_in = below - here
            step_x = pltpu.roll(here, C - 1, axis=0) - here
            return below, a * step_in + b * step_x, b * step_in + c * step_x

        def body(n, carry):
            here, above = carry
            for k in range(2):
                i = low + 2 * n + k
                below, flux_in, flux_x = flux(i, here)
                fresh = smooth[i] - ((above - flux_in) + (pltpu.roll(flux_x, 1, axis=0) - flux_x))
                store(dst, i, fresh)
                here, above = below, flux_in
            return here, above

        here, above, _ = flux(low - 1, src[plane, low - 1])
        lax.fori_loop(0, (high - low) // 2, body, (here, above))

    loads[0].wait()
    for q in range(3):
        xs[0][VECTORS + q, H:H + I, 0:J] = raw[q].astype(jnp.float32) * DAMPING
    loads[1].wait()
    pack(0, planes_of(0, 0))
    pl.semaphore_wait(barrier, neighbours)
    send(0, 0)
    loads[2].wait()
    pack(0, planes_of(0, 1))
    send(0, 1)

    row = lax.broadcasted_iota(jnp.int32, (S, S), 0)
    col = lax.broadcasted_iota(jnp.int32, (S, S), 1)
    taps = wavelet.shape[0]
    offset = col - row + taps // 2
    band = jnp.zeros((S, S), jnp.float32)
    for k in range(taps):
        band = jnp.where(offset == k, wavelet[k], band)
    gram = lax.dot_general(
        band, band, (((1,), (1,)), ((), ())),
        precision=lax.Precision.HIGHEST, preferred_element_type=jnp.float32,
    )
    whole = jnp.where(row == col, jnp.float32(1.0), jnp.float32(0.0)) - DAMPING * gram
    top = whole.astype(jnp.bfloat16)
    rest = (whole - top.astype(jnp.float32)).astype(jnp.bfloat16)
    for k in range(2):
        mat[k * S:(k + 1) * S, 0:S] = top
        mat[k * S:(k + 1) * S, S:2 * S] = rest

    for r in range(ROUNDS):
        for group in range(2):
            plane = 1 - group
            receive(r, group)
            src = xs[r]
            for k in range(1, H + 1):
                extra = H - k
                low, high = H - extra, H + I + extra
                last = k == H
                if not last:
                    dst = ys[r * (H - 1) + k - 1]

                    def store(dst, i, value):
                        dst[plane, i] = value
                elif r < ROUNDS - 1:
                    dst = xs[r + 1]

                    def store(dst, i, value):
                        dst[plane, i, 0:J] = value[0:J]
                        west_out[r + 1][plane, i - H] = value[0:H]
                        east_out[r + 1][plane, i - H] = value[J - H:J]
                else:
                    dst = out

                    def store(dst, i, value):
                        dst[group, i - H] = value[0:J]
                step(src, dst, plane, low, high, store)
                if not last:
                    @pl.when(jnp.logical_not(has[(1, 0)]))
                    def _():
                        dst[plane, H + I:high] = jnp.zeros((extra, C, S), jnp.float32)

                    @pl.when(jnp.logical_not(has[(0, 1)]))
                    def _():
                        dst[plane, low:high, J:J + extra] = jnp.zeros((high - low, extra, S), jnp.float32)
                src = dst
            if r < ROUNDS - 1:
                send(r + 1, group)

    for r in range(ROUNDS):
        for group in range(2):
            made = copies(r, group, planes_of(r, group))
            for way in WAYS:
                @pl.when(has[way])
                def _(way=way):
                    made[way].wait_send()


def per_device(probes, diffusion, wavelet):
    nv, I, J, S = probes.shape
    H = WIDTH
    C = J + SUB
    R = I + 2 * H
    f32 = jnp.float32
    planes = [PLANES] + [VECTORS] * (ROUNDS - 1)
    scratch = (
        [pltpu.VMEM((p, R, C, S), f32) for p in planes]
        + [pltpu.VMEM((VECTORS, R, C, S), f32) for _ in range(ROUNDS * (H - 1))]
        + [pltpu.VMEM((p, I, H, S), f32) for p in planes] * 2
        + [pltpu.VMEM((p, R, H, S), f32) for p in planes] * 2
        + [
            pltpu.VMEM(diffusion.shape, diffusion.dtype),
            pltpu.VMEM((R, C, S), f32),
            pltpu.VMEM((2 * S, 2 * S), jnp.bfloat16),
            pltpu.SemaphoreType.DMA((3,)),
            pltpu.SemaphoreType.DMA((ROUNDS, 2, len(WAYS))),
            pltpu.SemaphoreType.DMA((ROUNDS, 2, len(WAYS))),
        ]
    )
    return pl.pallas_call(
        kernel,
        out_shape=jax.ShapeDtypeStruct(probes.shape, f32),
        in_specs=[
            pl.BlockSpec(memory_space=pl.ANY),
            pl.BlockSpec(memory_space=pl.ANY),
            pl.BlockSpec(memory_space=pltpu.SMEM),
        ],
        out_specs=pl.BlockSpec(memory_space=pltpu.VMEM),
        scratch_shapes=scratch,
        compiler_params=pltpu.CompilerParams(
            collective_id=0, has_side_effects=True, vmem_limit_bytes=32 * 1024 * 1024
        ),
        cost_estimate=pl.CostEstimate(flops=STEPS * 2 * 1024 * 256 * 256, bytes_accessed=1500000, transcendentals=0),
    )(probes, diffusion, wavelet)


def solution(mesh):
    return jax.shard_map(
        per_device,
        mesh=mesh,
        in_specs=(P(None, "inline", "xline", None), P(None, "inline", "xline", None), P()),
        out_specs=P(None, "inline", "xline", None),
        check_vma=False,
    )
```

```python
import functools

import jax
import jax.numpy as jnp
from jax import lax
from jax.experimental import pallas as pl
from jax.experimental.pallas import tpu as pltpu
from jax.sharding import PartitionSpec as P

STEPS = 6
WIDTH = 2
ROUNDS = STEPS // WIDTH
DAMPING = 0.25
VECTORS = 2
PLANES = VECTORS + 3
SUB = 8
TILE = 16
WAYS = ((-1, 0), (1, 0), (0, -1), (0, 1), (-1, -1), (-1, 1), (1, -1), (1, 1))


def kernel(probes, diffusion, wavelet, out, *scratch):
    H = WIDTH
    nv, I, J, S = probes.shape
    C = J + SUB
    R = I + 2 * H
    f32, bf16 = jnp.float32, jnp.bfloat16
    at = 0

    def take(count):
        nonlocal at
        at += count
        return scratch[at - count:at]

    xs = take(ROUNDS)
    ys = take(ROUNDS * (H - 1))
    made_side = (take(1)[0], take(1)[0])
    sent_side = (take(ROUNDS), take(ROUNDS))
    west_in = take(ROUNDS)
    east_in = take(ROUNDS)
    corner_in = take(ROUNDS)
    raw, raw_in, smooth, mat, weights, load_sem, send_sem, recv_sem = take(8)
    WEST, EAST = 0, 1

    me_in = lax.axis_index("inline")
    me_x = lax.axis_index("xline")
    n_in = lax.axis_size("inline")
    n_x = lax.axis_size("xline")
    has = {
        (-1, 0): me_in > 0,
        (1, 0): me_in < n_in - 1,
        (0, -1): me_x > 0,
        (0, 1): me_x < n_x - 1,
    }
    for di, dx in WAYS[4:]:
        has[(di, dx)] = jnp.logical_and(has[(di, 0)], has[(0, dx)])

    def device(way):
        return {"inline": me_in + way[0], "xline": me_x + way[1]}

    loads = [
        pltpu.make_async_copy(diffusion, raw, load_sem.at[0]),
        pltpu.make_async_copy(probes.at[0], xs[0].at[1, H:H + I, 0:J], load_sem.at[1]),
        pltpu.make_async_copy(probes.at[1], xs[0].at[0, H:H + I, 0:J], load_sem.at[2]),
        pltpu.make_async_copy(wavelet, weights, load_sem.at[3]),
    ]
    for load in loads:
        load.start()

    barrier = pltpu.get_barrier_semaphore()
    for way in WAYS:
        @pl.when(has[way])
        def _(way=way):
            pl.semaphore_signal(
                barrier, inc=1, device_id=device(way), device_id_type=pl.DeviceIdType.MESH
            )

    for side, rows, corners, edge in (
        ((-1, 0), slice(0, H), (0, 1), 0),
        ((1, 0), slice(H + I, R), (2, 3), 1),
    ):
        @pl.when(jnp.logical_not(has[side]))
        def _(rows=rows, corners=corners, edge=edge):
            raw_in[edge] = jnp.zeros(raw_in.shape[1:], bf16)
            for r in range(ROUNDS):
                xs[r][0:VECTORS, rows, 0:J] = jnp.zeros((VECTORS, H, J, S), f32)
                for corner in corners:
                    corner_in[r][corner] = jnp.zeros(corner_in[r].shape[1:], bf16)
    for side, buffers, corners in (((0, 1), east_in, (1, 3)), ((0, -1), west_in, (0, 2))):
        @pl.when(jnp.logical_not(has[side]))
        def _(buffers=buffers, corners=corners):
            for r in range(ROUNDS):
                buffers[r][...] = jnp.zeros(buffers[r].shape, bf16)
                for corner in corners:
                    corner_in[r][corner] = jnp.zeros(corner_in[r].shape[1:], bf16)

    neighbours = (
        (1 + has[(-1, 0)].astype(jnp.int32) + has[(1, 0)].astype(jnp.int32))
        * (1 + has[(0, -1)].astype(jnp.int32) + has[(0, 1)].astype(jnp.int32))
        - 1
    )

    def planes_of(r, group):
        if group == 1:
            return (0, 1)
        return (1, PLANES) if r == 0 else (1, 2)

    def copies(r, group):
        x = xs[r]
        p = slice(*planes_of(r, group))
        vector = 1 - group
        west, east = sent_side[WEST][r], sent_side[EAST][r]
        count = I * H
        first, final = slice(0, TILE), slice(count - TILE, count)
        ends = [
            ((-1, 0), x.at[vector, H:2 * H, 0:J], x.at[vector, H + I:R, 0:J]),
            ((1, 0), x.at[vector, I:I + H, 0:J], x.at[vector, 0:H, 0:J]),
            ((0, -1), west.at[p], east_in[r].at[p]),
            ((0, 1), east.at[p], west_in[r].at[p]),
            ((-1, -1), west.at[p, first], corner_in[r].at[3, p]),
            ((-1, 1), east.at[p, first], corner_in[r].at[2, p]),
            ((1, -1), west.at[p, final], corner_in[r].at[1, p]),
            ((1, 1), east.at[p, final], corner_in[r].at[0, p]),
        ]
        if r == 0 and group == 0:
            ends += [
                ((-1, 0), raw.at[:, 0:H], raw_in.at[1]),
                ((1, 0), raw.at[:, I - H:I], raw_in.at[0]),
            ]
        return [
            (
                way,
                pltpu.make_async_remote_copy(
                    src_ref=source,
                    dst_ref=target,
                    send_sem=send_sem.at[r, group, k],
                    recv_sem=recv_sem.at[r, group, k],
                    device_id=device(way),
                    device_id_type=pl.DeviceIdType.MESH,
                ),
            )
            for k, (way, source, target) in enumerate(ends)
        ]

    def send(r, group):
        for p in range(*planes_of(r, group)):
            for side in (WEST, EAST):
                sent_side[side][r][p] = made_side[side][p].astype(bf16)
        for way, copy in copies(r, group):
            @pl.when(has[way])
            def _(copy=copy):
                copy.start()

    def pack(planes):
        for p in range(*planes):
            for i in range(I):
                made_side[WEST][p, i * H:(i + 1) * H] = xs[0][p, H + i, 0:H]
                made_side[EAST][p, i * H:(i + 1) * H] = xs[0][p, H + i, J - H:J]

    def receive(r, group):
        for way, copy in copies(r, group):
            @pl.when(has[(-way[0], -way[1])])
            def _(copy=copy):
                copy.wait_recv()
        x = xs[r]
        if r == 0 and group == 0:
            for edge, row in ((0, 0), (1, H + I)):
                x[VECTORS:PLANES, row:row + H, 0:J] = raw_in[edge].astype(f32) * DAMPING
        for p in range(*planes_of(r, group)):
            for column, middle, north, south in (
                (J, east_in[r], 1, 3),
                (C - H, west_in[r], 0, 2),
            ):
                main = middle[p].astype(f32)
                upper = corner_in[r][north, p].astype(f32)
                lower = corner_in[r][south, p].astype(f32)
                for i in range(I):
                    x[p, H + i, column:column + H] = main[i * H:(i + 1) * H]
                for i in range(H):
                    start = TILE - H * H + i * H
                    x[p, i, column:column + H] = upper[start:start + H]
                    x[p, H + I + i, column:column + H] = lower[i * H:(i + 1) * H]

    def product(block):
        top = block.astype(bf16)
        rest = (block - top.astype(f32)).astype(bf16)
        both = jnp.dot(
            jnp.concatenate([top, rest], axis=1), mat[...], preferred_element_type=f32
        )
        return both[:, :S] + both[:, S:]

    def smooth_own(src, plane):
        block = src[plane, H:H + I, 0:J].reshape(I * J, S)
        smooth[plane, H:H + I, 0:J] = product(block).reshape(I, J, S)

    def smooth_rest(src, plane, low, high):
        before, after = H - low, high - H - I
        pieces = [
            src[plane, low:H, 0:J].reshape(before * J, S),
            src[plane, H + I:high, 0:J].reshape(after * J, S),
            src[plane, low:high, J:C].reshape((high - low) * SUB, S),
        ]
        result = product(jnp.concatenate(pieces, axis=0))
        a, b = before * J, (before + after) * J
        smooth[plane, low:H, 0:J] = result[:a].reshape(before, J, S)
        smooth[plane, H + I:high, 0:J] = result[a:b].reshape(after, J, S)
        smooth[plane, low:high, J:C] = result[b:].reshape(high - low, SUB, S)

    def stencil(src, plane, low, high, store):
        tensor = xs[0]

        def flux(i, here):
            below = src[plane, i + 1]
            a, b, c = tensor[VECTORS, i], tensor[VECTORS + 1, i], tensor[VECTORS + 2, i]
            step_in = below - here
            step_x = pltpu.roll(here, C - 1, axis=0) - here
            return below, a * step_in + b * step_x, b * step_in + c * step_x

        here, above, _ = flux(low - 1, src[plane, low - 1])
        for i in range(low, high):
            below, flux_in, flux_x = flux(i, here)
            regular = (above - flux_in) + (pltpu.roll(flux_x, 1, axis=0) - flux_x)
            store(i, regular)
            here, above = below, flux_in

    loads[0].wait()
    for q in range(3):
        xs[0][VECTORS + q, H:H + I, 0:J] = raw[q].astype(f32) * DAMPING
    loads[1].wait()
    pack(planes_of(0, 0))
    pl.semaphore_wait(barrier, neighbours)
    send(0, 0)
    loads[2].wait()
    pack(planes_of(0, 1))
    send(0, 1)
    row = lax.broadcasted_iota(jnp.int32, (S, S), 0)
    col = lax.broadcasted_iota(jnp.int32, (S, S), 1)
    taps = wavelet.shape[0]
    offset = col - row + taps // 2
    loads[3].wait()
    band = jnp.zeros((S, S), f32)
    for k in range(taps):
        band = jnp.where(offset == k, weights[k], band)
    gram = lax.dot_general(
        band, band, (((1,), (1,)), ((), ())),
        precision=lax.Precision.HIGHEST, preferred_element_type=f32,
    )
    whole = jnp.where(row == col, f32(1.0), f32(0.0)) - DAMPING * gram
    top = whole.astype(bf16)
    rest = (whole - top.astype(f32)).astype(bf16)
    for k in range(2):
        mat[k * S:(k + 1) * S, 0:S] = top
        mat[k * S:(k + 1) * S, S:2 * S] = rest

    for group in range(2):
        smooth_own(xs[0], 1 - group)
    for r in range(ROUNDS):
        for group in range(2):
            plane = 1 - group
            receive(r, group)
            src = xs[r]
            for k in range(1, H + 1):
                extra = H - k
                low, high = H - extra, H + I + extra
                last = k == H
                if k > 1:
                    smooth_own(src, plane)
                if not last:
                    smooth_rest(src, plane, low, high)
                    dst = ys[r * (H - 1) + k - 1]

                    def store(i, regular):
                        dst[plane, i] = smooth[plane, i] - regular
                else:
                    def store(i, regular):
                        value = smooth[plane, i, 0:J] - regular[0:J]
                        if r == ROUNDS - 1:
                            out[group, i - H] = value
                            return
                        xs[r + 1][plane, i, 0:J] = value
                        place = slice((i - H) * H, (i - H + 1) * H)
                        made_side[WEST][plane, place] = value[0:H]
                        made_side[EAST][plane, place] = value[J - H:J]
                stencil(src, plane, low, high, store)
                if not last:
                    @pl.when(jnp.logical_not(has[(1, 0)]))
                    def _():
                        dst[plane, H + I:high] = jnp.zeros((extra, C, S), f32)

                    @pl.when(jnp.logical_not(has[(0, 1)]))
                    def _():
                        dst[plane, low:high, J:J + extra] = jnp.zeros((high - low, extra, S), f32)
                    src = dst
            if r < ROUNDS - 1:
                send(r + 1, group)
                smooth_own(xs[r + 1], plane)

    for r in range(ROUNDS):
        for group in range(2):
            for way, copy in copies(r, group):
                @pl.when(has[way])
                def _(copy=copy):
                    copy.wait_send()


def per_device(probes, diffusion, wavelet):
    nv, I, J, S = probes.shape
    H = WIDTH
    C = J + SUB
    R = I + 2 * H
    f32 = jnp.float32
    planes = [PLANES] + [VECTORS] * (ROUNDS - 1)
    bf16 = jnp.bfloat16
    scratch = (
        [pltpu.VMEM((p, R, C, S), f32) for p in planes]
        + [pltpu.VMEM((VECTORS, R, C, S), f32) for _ in range(ROUNDS * (H - 1))]
        + [pltpu.VMEM((PLANES, I * H, S), f32)] * 2
        + [pltpu.VMEM((p, I * H, S), bf16) for p in planes] * 4
        + [pltpu.VMEM((4, p, TILE, S), bf16) for p in planes]
        + [
            pltpu.VMEM(diffusion.shape, diffusion.dtype),
            pltpu.VMEM((2, 3, H, J, S), bf16),
            pltpu.VMEM((VECTORS, R, C, S), f32),
            pltpu.VMEM((2 * S, 2 * S), bf16),
            pltpu.SMEM(wavelet.shape, f32),
            pltpu.SemaphoreType.DMA((4,)),
            pltpu.SemaphoreType.DMA((ROUNDS, 2, len(WAYS) + 2)),
            pltpu.SemaphoreType.DMA((ROUNDS, 2, len(WAYS) + 2)),
        ]
    )
    return pl.pallas_call(
        kernel,
        out_shape=jax.ShapeDtypeStruct(probes.shape, f32),
        in_specs=[
            pl.BlockSpec(memory_space=pltpu.HBM),
            pl.BlockSpec(memory_space=pltpu.HBM),
            pl.BlockSpec(memory_space=pltpu.HBM),
        ],
        out_specs=pl.BlockSpec(memory_space=pltpu.VMEM),
        scratch_shapes=scratch,
        compiler_params=pltpu.CompilerParams(
            collective_id=0, has_side_effects=True, vmem_limit_bytes=32 * 1024 * 1024
        ),
        cost_estimate=pl.CostEstimate(flops=STEPS * 2 * 1024 * 256 * 256, bytes_accessed=1500000, transcendentals=0),
    )(probes, diffusion, wavelet)


def solution(mesh):
    return jax.shard_map(
        per_device,
        mesh=mesh,
        in_specs=(P(None, "inline", "xline", None), P(None, "inline", "xline", None), P()),
        out_specs=P(None, "inline", "xline", None),
        check_vma=False,
    )
```

```python
import functools

import jax
import jax.numpy as jnp
from jax import lax
from jax.experimental import pallas as pl
from jax.experimental.pallas import tpu as pltpu
from jax.sharding import PartitionSpec as P

STEPS = 6
WIDTH = 3
ROUNDS = STEPS // WIDTH
DAMPING = 0.25
VECTORS = 2
PLANES = VECTORS + 3
SUB = 8
TILE = 16
WAYS = ((-1, 0), (1, 0), (0, -1), (0, 1), (-1, -1), (-1, 1), (1, -1), (1, 1))


def kernel(probes, diffusion, wavelet, out, *scratch):
    H = WIDTH
    nv, I, J, S = probes.shape
    C = J + SUB
    R = I + 2 * H
    f32, bf16 = jnp.float32, jnp.bfloat16
    at = 0

    def take(count):
        nonlocal at
        at += count
        return scratch[at - count:at]

    xs = take(ROUNDS)
    ys = take(ROUNDS * (H - 1))
    made_side = (take(1)[0], take(1)[0])
    sent_side = (take(ROUNDS), take(ROUNDS))
    west_in = take(ROUNDS)
    east_in = take(ROUNDS)
    corner_in = take(ROUNDS)
    raw, raw_in, smooth, mat, weights, load_sem, send_sem, recv_sem = take(8)
    WEST, EAST = 0, 1

    me_in = lax.axis_index("inline")
    me_x = lax.axis_index("xline")
    n_in = lax.axis_size("inline")
    n_x = lax.axis_size("xline")
    has = {
        (-1, 0): me_in > 0,
        (1, 0): me_in < n_in - 1,
        (0, -1): me_x > 0,
        (0, 1): me_x < n_x - 1,
    }
    for di, dx in WAYS[4:]:
        has[(di, dx)] = jnp.logical_and(has[(di, 0)], has[(0, dx)])

    def device(way):
        return {"inline": me_in + way[0], "xline": me_x + way[1]}

    loads = [
        pltpu.make_async_copy(diffusion, raw, load_sem.at[0]),
        pltpu.make_async_copy(probes.at[0], xs[0].at[1, H:H + I, 0:J], load_sem.at[1]),
        pltpu.make_async_copy(probes.at[1], xs[0].at[0, H:H + I, 0:J], load_sem.at[2]),
        pltpu.make_async_copy(wavelet, weights, load_sem.at[3]),
    ]
    for load in loads:
        load.start()

    barrier = pltpu.get_barrier_semaphore()
    for way in WAYS:
        @pl.when(has[way])
        def _(way=way):
            pl.semaphore_signal(
                barrier, inc=1, device_id=device(way), device_id_type=pl.DeviceIdType.MESH
            )

    neighbours = (
        (1 + has[(-1, 0)].astype(jnp.int32) + has[(1, 0)].astype(jnp.int32))
        * (1 + has[(0, -1)].astype(jnp.int32) + has[(0, 1)].astype(jnp.int32))
        - 1
    )

    def planes_of(r, group):
        if group == 1:
            return (0, 1)
        return (1, PLANES) if r == 0 else (1, 2)

    def copies(r, group):
        x = xs[r]
        p = slice(*planes_of(r, group))
        vector = 1 - group
        west, east = sent_side[WEST][r], sent_side[EAST][r]
        count = I * H
        first, final = slice(0, TILE), slice(count - TILE, count)
        ends = [
            ((-1, -1), west.at[p, first], corner_in[r].at[3, p]),
            ((-1, 1), east.at[p, first], corner_in[r].at[2, p]),
            ((1, -1), west.at[p, final], corner_in[r].at[1, p]),
            ((1, 1), east.at[p, final], corner_in[r].at[0, p]),
            ((0, -1), west.at[p], east_in[r].at[p]),
            ((0, 1), east.at[p], west_in[r].at[p]),
            ((-1, 0), x.at[vector, H:2 * H, 0:J], x.at[vector, H + I:R, 0:J]),
            ((1, 0), x.at[vector, I:I + H, 0:J], x.at[vector, 0:H, 0:J]),
        ]
        if r == 0 and group == 0:
            ends += [
                ((-1, 0), raw.at[:, 0:H], raw_in.at[1]),
                ((1, 0), raw.at[:, I - H:I], raw_in.at[0]),
            ]
        return [
            (
                way,
                pltpu.make_async_remote_copy(
                    src_ref=source,
                    dst_ref=target,
                    send_sem=send_sem.at[r, group, k],
                    recv_sem=recv_sem.at[r, group, k],
                    device_id=device(way),
                    device_id_type=pl.DeviceIdType.MESH,
                ),
            )
            for k, (way, source, target) in enumerate(ends)
        ]

    def send(r, group):
        for p in range(*planes_of(r, group)):
            for side in (WEST, EAST):
                sent_side[side][r][p] = made_side[side][p].astype(bf16)
        for way, copy in copies(r, group):
            @pl.when(has[way])
            def _(copy=copy):
                copy.start()

    def pack(planes):
        for p in range(*planes):
            for i in range(I):
                made_side[WEST][p, i * H:(i + 1) * H] = xs[0][p, H + i, 0:H]
                made_side[EAST][p, i * H:(i + 1) * H] = xs[0][p, H + i, J - H:J]

    def receive(r, group):
        for way, copy in copies(r, group):
            @pl.when(has[(-way[0], -way[1])])
            def _(copy=copy):
                copy.wait_recv()
        x = xs[r]
        if r == 0 and group == 0:
            for edge, row in ((0, 0), (1, H + I)):
                x[VECTORS:PLANES, row:row + H, 0:J] = raw_in[edge].astype(f32) * DAMPING
        for p in range(*planes_of(r, group)):
            for column, middle, north, south in (
                (J, east_in[r], 1, 3),
                (C - H, west_in[r], 0, 2),
            ):
                main = middle[p].astype(f32)
                upper = corner_in[r][north, p].astype(f32)
                lower = corner_in[r][south, p].astype(f32)
                for i in range(I):
                    x[p, H + i, column:column + H] = main[i * H:(i + 1) * H]
                for i in range(H):
                    start = TILE - H * H + i * H
                    x[p, i, column:column + H] = upper[start:start + H]
                    x[p, H + I + i, column:column + H] = lower[i * H:(i + 1) * H]

    def product(block):
        top = block.astype(bf16)
        rest = (block - top.astype(f32)).astype(bf16)
        both = jnp.dot(
            jnp.concatenate([top, rest], axis=1), mat[...], preferred_element_type=f32
        )
        return both[:, :S] + both[:, S:]

    def smooth_own(src, plane):
        block = src[plane, H:H + I, 0:J].reshape(I * J, S)
        smooth[plane, H:H + I, 0:J] = product(block).reshape(I, J, S)

    def smooth_rest(src, plane, low, high):
        before, after = H - low, high - H - I
        pieces = [
            src[plane, low:H, 0:J].reshape(before * J, S),
            src[plane, H + I:high, 0:J].reshape(after * J, S),
            src[plane, low:high, J:C].reshape((high - low) * SUB, S),
        ]
        result = product(jnp.concatenate(pieces, axis=0))
        a, b = before * J, (before + after) * J
        smooth[plane, low:H, 0:J] = result[:a].reshape(before, J, S)
        smooth[plane, H + I:high, 0:J] = result[a:b].reshape(after, J, S)
        smooth[plane, low:high, J:C] = result[b:].reshape(high - low, SUB, S)

    def stencil(src, plane, low, high, store):
        tensor = xs[0]

        def flux(i, here):
            below = src[plane, i + 1]
            a, b, c = tensor[VECTORS, i], tensor[VECTORS + 1, i], tensor[VECTORS + 2, i]
            step_in = below - here
            step_x = pltpu.roll(here, C - 1, axis=0) - here
            return below, a * step_in + b * step_x, b * step_in + c * step_x

        here, above, _ = flux(low - 1, src[plane, low - 1])
        for i in range(low, high):
            below, flux_in, flux_x = flux(i, here)
            regular = (above - flux_in) + (pltpu.roll(flux_x, 1, axis=0) - flux_x)
            store(i, regular)
            here, above = below, flux_in

    loads[0].wait()
    for q in range(3):
        xs[0][VECTORS + q, H:H + I, 0:J] = raw[q].astype(f32) * DAMPING
    loads[1].wait()
    pack(planes_of(0, 0))
    pl.semaphore_wait(barrier, neighbours)
    send(0, 0)
    loads[2].wait()
    pack(planes_of(0, 1))
    send(0, 1)
    for side, rows, corners, edge in (
        ((-1, 0), slice(0, H), (0, 1), 0),
        ((1, 0), slice(H + I, R), (2, 3), 1),
    ):
        @pl.when(jnp.logical_not(has[side]))
        def _(rows=rows, corners=corners, edge=edge):
            raw_in[edge] = jnp.zeros(raw_in.shape[1:], bf16)
            for r in range(ROUNDS):
                xs[r][0:VECTORS, rows, 0:J] = jnp.zeros((VECTORS, H, J, S), f32)
                for corner in corners:
                    corner_in[r][corner] = jnp.zeros(corner_in[r].shape[1:], bf16)
    for side, buffers, corners in (((0, 1), east_in, (1, 3)), ((0, -1), west_in, (0, 2))):
        @pl.when(jnp.logical_not(has[side]))
        def _(buffers=buffers, corners=corners):
            for r in range(ROUNDS):
                buffers[r][...] = jnp.zeros(buffers[r].shape, bf16)
                for corner in corners:
                    corner_in[r][corner] = jnp.zeros(corner_in[r].shape[1:], bf16)

    row = lax.broadcasted_iota(jnp.int32, (S, S), 0)
    col = lax.broadcasted_iota(jnp.int32, (S, S), 1)
    taps = wavelet.shape[0]
    offset = col - row + taps // 2
    loads[3].wait()
    band = jnp.zeros((S, S), f32)
    for k in range(taps):
        band = jnp.where(offset == k, weights[k], band)
    gram = lax.dot_general(
        band, band, (((1,), (1,)), ((), ())),
        precision=lax.Precision.HIGHEST, preferred_element_type=f32,
    )
    whole = jnp.where(row == col, f32(1.0), f32(0.0)) - DAMPING * gram
    top = whole.astype(bf16)
    rest = (whole - top.astype(f32)).astype(bf16)
    for k in range(2):
        mat[k * S:(k + 1) * S, 0:S] = top
        mat[k * S:(k + 1) * S, S:2 * S] = rest

    for group in range(2):
        smooth_own(xs[0], 1 - group)
    for r in range(ROUNDS):
        for group in range(2):
            plane = 1 - group
            receive(r, group)
            src = xs[r]
            for k in range(1, H + 1):
                extra = H - k
                low, high = H - extra, H + I + extra
                last = k == H
                if k > 1:
                    smooth_own(src, plane)
                if not last:
                    smooth_rest(src, plane, low, high)
                    dst = ys[r * (H - 1) + k - 1]

                    def store(i, regular):
                        dst[plane, i] = smooth[plane, i] - regular
                else:
                    def store(i, regular):
                        value = smooth[plane, i, 0:J] - regular[0:J]
                        if r == ROUNDS - 1:
                            out[group, i - H] = value
                            return
                        xs[r + 1][plane, i, 0:J] = value
                        place = slice((i - H) * H, (i - H + 1) * H)
                        made_side[WEST][plane, place] = value[0:H]
                        made_side[EAST][plane, place] = value[J - H:J]
                stencil(src, plane, low, high, store)
                if not last:
                    @pl.when(jnp.logical_not(has[(1, 0)]))
                    def _():
                        dst[plane, H + I:high] = jnp.zeros((extra, C, S), f32)

                    @pl.when(jnp.logical_not(has[(0, 1)]))
                    def _():
                        dst[plane, low:high, J:J + extra] = jnp.zeros((high - low, extra, S), f32)
                    src = dst
            if r < ROUNDS - 1:
                send(r + 1, group)
                smooth_own(xs[r + 1], plane)

    for r in range(ROUNDS):
        for group in range(2):
            for way, copy in copies(r, group):
                @pl.when(has[way])
                def _(copy=copy):
                    copy.wait_send()


def per_device(probes, diffusion, wavelet):
    nv, I, J, S = probes.shape
    H = WIDTH
    C = J + SUB
    R = I + 2 * H
    f32 = jnp.float32
    planes = [PLANES] + [VECTORS] * (ROUNDS - 1)
    bf16 = jnp.bfloat16
    scratch = (
        [pltpu.VMEM((p, R, C, S), f32) for p in planes]
        + [pltpu.VMEM((VECTORS, R, C, S), f32) for _ in range(ROUNDS * (H - 1))]
        + [pltpu.VMEM((PLANES, I * H, S), f32)] * 2
        + [pltpu.VMEM((p, I * H, S), bf16) for p in planes] * 4
        + [pltpu.VMEM((4, p, TILE, S), bf16) for p in planes]
        + [
            pltpu.VMEM(diffusion.shape, diffusion.dtype),
            pltpu.VMEM((2, 3, H, J, S), bf16),
            pltpu.VMEM((VECTORS, R, C, S), f32),
            pltpu.VMEM((2 * S, 2 * S), bf16),
            pltpu.SMEM(wavelet.shape, f32),
            pltpu.SemaphoreType.DMA((4,)),
            pltpu.SemaphoreType.DMA((ROUNDS, 2, len(WAYS) + 2)),
            pltpu.SemaphoreType.DMA((ROUNDS, 2, len(WAYS) + 2)),
        ]
    )
    return pl.pallas_call(
        kernel,
        out_shape=jax.ShapeDtypeStruct(probes.shape, f32),
        in_specs=[
            pl.BlockSpec(memory_space=pltpu.HBM),
            pl.BlockSpec(memory_space=pltpu.HBM),
            pl.BlockSpec(memory_space=pltpu.HBM),
        ],
        out_specs=pl.BlockSpec(memory_space=pltpu.VMEM),
        scratch_shapes=scratch,
        compiler_params=pltpu.CompilerParams(
            collective_id=0, has_side_effects=True, vmem_limit_bytes=32 * 1024 * 1024
        ),
        cost_estimate=pl.CostEstimate(flops=STEPS * 2 * 1024 * 256 * 256, bytes_accessed=1500000, transcendentals=0),
    )(probes, diffusion, wavelet)


def solution(mesh):
    return jax.shard_map(
        per_device,
        mesh=mesh,
        in_specs=(P(None, "inline", "xline", None), P(None, "inline", "xline", None), P()),
        out_specs=P(None, "inline", "xline", None),
        check_vma=False,
    )
```

```python
import functools

import jax
import jax.numpy as jnp
from jax import lax
from jax.experimental import pallas as pl
from jax.experimental.pallas import tpu as pltpu
from jax.sharding import PartitionSpec as P

STEPS = 6
WIDTH = 3
ROUNDS = STEPS // WIDTH
DAMPING = 0.25
VECTORS = 2
PLANES = VECTORS + 3
SUB = 8
TILE = 16
WAYS = ((-1, 0), (1, 0), (0, -1), (0, 1), (-1, -1), (-1, 1), (1, -1), (1, 1))


def kernel(probes, diffusion, wavelet, out, *scratch):
    H = WIDTH
    nv, I, J, S = probes.shape
    C = J + SUB
    R = I + 2 * H
    f32, bf16 = jnp.float32, jnp.bfloat16
    at = 0

    def take(count):
        nonlocal at
        at += count
        return scratch[at - count:at]

    xs = take(ROUNDS)
    ys = take(ROUNDS * (H - 1))
    made_side = (take(1)[0], take(1)[0])
    sent_side = (take(ROUNDS), take(ROUNDS))
    west_in = take(ROUNDS)
    east_in = take(ROUNDS)
    corner_in = take(ROUNDS)
    raw, raw_in, smooth, mat, weights, load_sem, send_sem, recv_sem = take(8)
    WEST, EAST = 0, 1

    me_in = lax.axis_index("inline")
    me_x = lax.axis_index("xline")
    n_in = lax.axis_size("inline")
    n_x = lax.axis_size("xline")
    has = {
        (-1, 0): me_in > 0,
        (1, 0): me_in < n_in - 1,
        (0, -1): me_x > 0,
        (0, 1): me_x < n_x - 1,
    }
    for di, dx in WAYS[4:]:
        has[(di, dx)] = jnp.logical_and(has[(di, 0)], has[(0, dx)])

    def device(way):
        return {"inline": me_in + way[0], "xline": me_x + way[1]}

    barrier = pltpu.get_barrier_semaphore()
    for way in WAYS[4:] + WAYS[:4]:
        @pl.when(has[way])
        def _(way=way):
            pl.semaphore_signal(
                barrier, inc=1, device_id=device(way), device_id_type=pl.DeviceIdType.MESH
            )

    loads = [
        pltpu.make_async_copy(diffusion, raw, load_sem.at[0]),
        pltpu.make_async_copy(probes.at[0], xs[0].at[1, H:H + I, 0:J], load_sem.at[1]),
        pltpu.make_async_copy(probes.at[1], xs[0].at[0, H:H + I, 0:J], load_sem.at[2]),
        pltpu.make_async_copy(wavelet, weights, load_sem.at[3]),
    ]
    for load in loads:
        load.start()

    neighbours = (
        (1 + has[(-1, 0)].astype(jnp.int32) + has[(1, 0)].astype(jnp.int32))
        * (1 + has[(0, -1)].astype(jnp.int32) + has[(0, 1)].astype(jnp.int32))
        - 1
    )

    def planes_of(r, group):
        if group == 1:
            return (0, 1)
        return (1, PLANES) if r == 0 else (1, 2)

    def copies(r, group):
        x = xs[r]
        p = slice(*planes_of(r, group))
        vector = 1 - group
        west, east = sent_side[WEST][r], sent_side[EAST][r]
        count = I * H
        first, final = slice(0, TILE), slice(count - TILE, count)
        ends = [
            ((-1, -1), west.at[p, first], corner_in[r].at[3, p]),
            ((-1, 1), east.at[p, first], corner_in[r].at[2, p]),
            ((1, -1), west.at[p, final], corner_in[r].at[1, p]),
            ((1, 1), east.at[p, final], corner_in[r].at[0, p]),
            ((0, -1), west.at[p], east_in[r].at[p]),
            ((0, 1), east.at[p], west_in[r].at[p]),
            ((-1, 0), x.at[vector, H:2 * H, 0:J], x.at[vector, H + I:R, 0:J]),
            ((1, 0), x.at[vector, I:I + H, 0:J], x.at[vector, 0:H, 0:J]),
        ]
        if r == 0 and group == 0:
            ends += [
                ((-1, 0), raw.at[:, 0:H], raw_in.at[1]),
                ((1, 0), raw.at[:, I - H:I], raw_in.at[0]),
            ]
        return [
            (
                way,
                pltpu.make_async_remote_copy(
                    src_ref=source,
                    dst_ref=target,
                    send_sem=send_sem.at[r, group, k],
                    recv_sem=recv_sem.at[r, group, k],
                    device_id=device(way),
                    device_id_type=pl.DeviceIdType.MESH,
                ),
            )
            for k, (way, source, target) in enumerate(ends)
        ]

    def send(r, group):
        for p in range(*planes_of(r, group)):
            for side in (WEST, EAST):
                sent_side[side][r][p] = made_side[side][p].astype(bf16)
        for way, copy in copies(r, group):
            @pl.when(has[way])
            def _(copy=copy):
                copy.start()

    def pack(planes):
        for p in range(*planes):
            for i in range(I):
                made_side[WEST][p, i * H:(i + 1) * H] = xs[0][p, H + i, 0:H]
                made_side[EAST][p, i * H:(i + 1) * H] = xs[0][p, H + i, J - H:J]

    def receive(r, group):
        arriving = copies(r, group)

        def wait(part):
            for way, copy in part:
                @pl.when(has[(-way[0], -way[1])])
                def _(copy=copy):
                    copy.wait_recv()

        x = xs[r]
        sides = ((J, east_in[r], 1, 3), (C - H, west_in[r], 0, 2))
        wait(arriving[6:])
        if r == 0 and group == 0:
            for edge, row in ((0, 0), (1, H + I)):
                x[VECTORS:PLANES, row:row + H, 0:J] = raw_in[edge].astype(f32) * DAMPING
        wait(arriving[4:6])
        for p in range(*planes_of(r, group)):
            for column, middle, north, south in sides:
                main = middle[p].astype(f32)
                for i in range(I):
                    x[p, H + i, column:column + H] = main[i * H:(i + 1) * H]
        wait(arriving[:4])
        for p in range(*planes_of(r, group)):
            for column, middle, north, south in sides:
                upper = corner_in[r][north, p].astype(f32)
                lower = corner_in[r][south, p].astype(f32)
                for i in range(H):
                    start = TILE - H * H + i * H
                    x[p, i, column:column + H] = upper[start:start + H]
                    x[p, H + I + i, column:column + H] = lower[i * H:(i + 1) * H]

    def product(block):
        top = block.astype(bf16)
        rest = (block - top.astype(f32)).astype(bf16)
        both = jnp.dot(
            jnp.concatenate([top, rest], axis=1), mat[...], preferred_element_type=f32
        )
        return both[:, :S] + both[:, S:]

    def smooth_own(src, plane):
        block = src[plane, H:H + I, 0:J].reshape(I * J, S)
        smooth[plane, H:H + I, 0:J] = product(block).reshape(I, J, S)

    def smooth_rest(src, plane, low, high):
        before, after = H - low, high - H - I
        pieces = [
            src[plane, low:H, 0:J].reshape(before * J, S),
            src[plane, H + I:high, 0:J].reshape(after * J, S),
            src[plane, low:high, J:C].reshape((high - low) * SUB, S),
        ]
        result = product(jnp.concatenate(pieces, axis=0))
        a, b = before * J, (before + after) * J
        smooth[plane, low:H, 0:J] = result[:a].reshape(before, J, S)
        smooth[plane, H + I:high, 0:J] = result[a:b].reshape(after, J, S)
        smooth[plane, low:high, J:C] = result[b:].reshape(high - low, SUB, S)

    def stencil(src, plane, low, high, store):
        tensor = xs[0]

        def flux(i, here):
            below = src[plane, i + 1]
            a, b, c = tensor[VECTORS, i], tensor[VECTORS + 1, i], tensor[VECTORS + 2, i]
            step_in = below - here
            step_x = pltpu.roll(here, C - 1, axis=0) - here
            return below, a * step_in + b * step_x, b * step_in + c * step_x

        here, above, _ = flux(low - 1, src[plane, low - 1])
        for i in range(low, high):
            below, flux_in, flux_x = flux(i, here)
            regular = (above - flux_in) + (pltpu.roll(flux_x, 1, axis=0) - flux_x)
            store(i, regular)
            here, above = below, flux_in

    loads[0].wait()
    for q in range(3):
        xs[0][VECTORS + q, H:H + I, 0:J] = raw[q].astype(f32) * DAMPING
    loads[1].wait()
    pack(planes_of(0, 0))
    pl.semaphore_wait(barrier, neighbours)
    send(0, 0)
    loads[2].wait()
    pack(planes_of(0, 1))
    send(0, 1)
    for side, rows, corners, edge in (
        ((-1, 0), slice(0, H), (0, 1), 0),
        ((1, 0), slice(H + I, R), (2, 3), 1),
    ):
        @pl.when(jnp.logical_not(has[side]))
        def _(rows=rows, corners=corners, edge=edge):
            raw_in[edge] = jnp.zeros(raw_in.shape[1:], bf16)
            for r in range(ROUNDS):
                xs[r][0:VECTORS, rows, 0:J] = jnp.zeros((VECTORS, H, J, S), f32)
                for corner in corners:
                    corner_in[r][corner] = jnp.zeros(corner_in[r].shape[1:], bf16)
    for side, buffers, corners in (((0, 1), east_in, (1, 3)), ((0, -1), west_in, (0, 2))):
        @pl.when(jnp.logical_not(has[side]))
        def _(buffers=buffers, corners=corners):
            for r in range(ROUNDS):
                buffers[r][...] = jnp.zeros(buffers[r].shape, bf16)
                for corner in corners:
                    corner_in[r][corner] = jnp.zeros(corner_in[r].shape[1:], bf16)

    row = lax.broadcasted_iota(jnp.int32, (S, S), 0)
    col = lax.broadcasted_iota(jnp.int32, (S, S), 1)
    taps = wavelet.shape[0]
    offset = col - row + taps // 2
    loads[3].wait()
    band = jnp.zeros((S, S), f32)
    for k in range(taps):
        band = jnp.where(offset == k, weights[k], band)
    gram = lax.dot_general(
        band, band, (((1,), (1,)), ((), ())),
        precision=lax.Precision.HIGHEST, preferred_element_type=f32,
    )
    whole = jnp.where(row == col, f32(1.0), f32(0.0)) - DAMPING * gram
    top = whole.astype(bf16)
    rest = (whole - top.astype(f32)).astype(bf16)
    for k in range(2):
        mat[k * S:(k + 1) * S, 0:S] = top
        mat[k * S:(k + 1) * S, S:2 * S] = rest

    for group in range(2):
        smooth_own(xs[0], 1 - group)
    for r in range(ROUNDS):
        for group in range(2):
            plane = 1 - group
            receive(r, group)
            src = xs[r]
            for k in range(1, H + 1):
                extra = H - k
                low, high = H - extra, H + I + extra
                last = k == H
                if k > 1:
                    smooth_own(src, plane)
                if not last:
                    smooth_rest(src, plane, low, high)
                    dst = ys[r * (H - 1) + k - 1]

                    def store(i, regular):
                        dst[plane, i] = smooth[plane, i] - regular
                else:
                    def store(i, regular):
                        value = smooth[plane, i, 0:J] - regular[0:J]
                        if r == ROUNDS - 1:
                            out[group, i - H] = value
                            return
                        xs[r + 1][plane, i, 0:J] = value
                        place = slice((i - H) * H, (i - H + 1) * H)
                        made_side[WEST][plane, place] = value[0:H]
                        made_side[EAST][plane, place] = value[J - H:J]
                stencil(src, plane, low, high, store)
                if not last:
                    @pl.when(jnp.logical_not(has[(1, 0)]))
                    def _():
                        dst[plane, H + I:high] = jnp.zeros((extra, C, S), f32)

                    @pl.when(jnp.logical_not(has[(0, 1)]))
                    def _():
                        dst[plane, low:high, J:J + extra] = jnp.zeros((high - low, extra, S), f32)
                    src = dst
            if r < ROUNDS - 1:
                send(r + 1, group)
                smooth_own(xs[r + 1], plane)

    for r in range(ROUNDS):
        for group in range(2):
            for way, copy in copies(r, group):
                @pl.when(has[way])
                def _(copy=copy):
                    copy.wait_send()


def per_device(probes, diffusion, wavelet):
    nv, I, J, S = probes.shape
    H = WIDTH
    C = J + SUB
    R = I + 2 * H
    f32 = jnp.float32
    planes = [PLANES] + [VECTORS] * (ROUNDS - 1)
    bf16 = jnp.bfloat16
    scratch = (
        [pltpu.VMEM((p, R, C, S), f32) for p in planes]
        + [pltpu.VMEM((VECTORS, R, C, S), f32) for _ in range(ROUNDS * (H - 1))]
        + [pltpu.VMEM((PLANES, I * H, S), f32)] * 2
        + [pltpu.VMEM((p, I * H, S), bf16) for p in planes] * 4
        + [pltpu.VMEM((4, p, TILE, S), bf16) for p in planes]
        + [
            pltpu.VMEM(diffusion.shape, diffusion.dtype),
            pltpu.VMEM((2, 3, H, J, S), bf16),
            pltpu.VMEM((VECTORS, R, C, S), f32),
            pltpu.VMEM((2 * S, 2 * S), bf16),
            pltpu.SMEM(wavelet.shape, f32),
            pltpu.SemaphoreType.DMA((4,)),
            pltpu.SemaphoreType.DMA((ROUNDS, 2, len(WAYS) + 2)),
            pltpu.SemaphoreType.DMA((ROUNDS, 2, len(WAYS) + 2)),
        ]
    )
    return pl.pallas_call(
        kernel,
        out_shape=jax.ShapeDtypeStruct(probes.shape, f32),
        in_specs=[
            pl.BlockSpec(memory_space=pltpu.HBM),
            pl.BlockSpec(memory_space=pltpu.HBM),
            pl.BlockSpec(memory_space=pltpu.HBM),
        ],
        out_specs=pl.BlockSpec(memory_space=pltpu.VMEM),
        scratch_shapes=scratch,
        compiler_params=pltpu.CompilerParams(
            collective_id=0, has_side_effects=True, vmem_limit_bytes=32 * 1024 * 1024
        ),
        cost_estimate=pl.CostEstimate(flops=STEPS * 2 * 1024 * 256 * 256, bytes_accessed=1500000, transcendentals=0),
    )(probes, diffusion, wavelet)


def solution(mesh):
    return jax.shard_map(
        per_device,
        mesh=mesh,
        in_specs=(P(None, "inline", "xline", None), P(None, "inline", "xline", None), P()),
        out_specs=P(None, "inline", "xline", None),
        check_vma=False,
    )
```
